512 devices in a mesh: dp: 2 (over y_lo), ctx: 32 (over z, y_hi), tp: 8 (over x, core).
Axes of the slice: x: 4, y: 4 (y_hi: 2, y_lo: 2; y = y_hi * 2 + y_lo), z: 16, core: 2. Of those that a mesh axis runs over, the one named last changes fastest.
Arguments:
- queries: bfloat16 [8192, 3072], P(('dp', 'ctx'), 'tp'), parts along dimension 0, may hold values from -6 to 6
- query_tangent: bfloat16 [8192, 3072], P(('dp', 'ctx'), 'tp'), parts along dimension 0, may hold values from -6 to 6
- key_rows: bfloat16 [8192, 3072], P(('dp', 'ctx'), 'tp'), parts along dimension 0, may hold values from -6 to 6
- key_tangent: bfloat16 [8192, 3072], P(('dp', 'ctx'), 'tp'), parts along dimension 0, may hold values from -6 to 6
- value_rows: bfloat16 [8192, 3072], P(('dp', 'ctx'), 'tp'), parts along dimension 0, may hold values from -6 to 6
- value_tangent: bfloat16 [8192, 3072], P(('dp', 'ctx'), 'tp'), parts along dimension 0, may hold values from -6 to 6
- out_weight: bfloat16 [3072, 5120], P('tp'), may hold values from -0.15625 to 0.15625
- out_bias: float32 [5120], P('tp'), may hold values from -3 to 3
- gate_scale: float32 [10240], P(('dp', 'tp')), parts along dimension 0, may hold values from 0.1 to 1.9
- gate_tangent: float32 [10240], P(('dp', 'tp')), parts along dimension 0, may hold values from -6 to 6
Outputs:
- block_output: bfloat16 [8192, 5120], P(('dp', 'ctx'), 'tp'), parts along dimension 0
- output_tangent: bfloat16 [8192, 5120], P(('dp', 'ctx'), 'tp'), parts along dimension 0
The draws below stay inside these ranges and needn't reach their ends.
There are 2 independent parts, one for each index of `dp`. The reference program is written for one: setup_inputs(seed, part) draws one part's arguments, and reference() takes and returns one part's arrays. A program takes and returns all parts, laid end to end along the dimension named above; an argument that names none is the same for every part. Nothing has to cross between parts.
All inputs are finite; a program needn't handle non-finite values.
Results may differ from the reference program's by a relative error of at most 0.02.
Values may be sent and summed in bfloat16 or wider, within the bound.
A program may use at most 64 MiB of HBM per device.

```python
import jax
import jax.numpy as jnp
from jax import lax

D = 5120
HD = 128
HEADS = 24
TOKENS = 4096
HQ = 3072
N_TP = 8


def draw_queries(key, part):
    key = jax.random.fold_in(key, 1)
    base = jnp.clip(1.6 * jax.random.normal(key, (TOKENS, HQ), jnp.float32), -6.0, 6.0)
    return base.astype(jnp.bfloat16)


def draw_key_rows(key, part):
    key = jax.random.fold_in(key, 2)
    base = jnp.clip(1.6 * jax.random.normal(key, (TOKENS, HQ), jnp.float32), -6.0, 6.0)
    return base.astype(jnp.bfloat16)


def strengthened(drawn, own_key, source, target, shards_of, factor):
    owner, partner = [(jnp.arange(drawn.shape[dim]) // (drawn.shape[dim] // shards_of)).reshape([-1 if axis == dim else 1 for axis in range(drawn.ndim)]) for dim in (source, target)]
    chosen = jax.random.permutation(own_key, shards_of)[partner]
    strong = (owner == chosen) | (owner == (partner + shards_of // 2) % shards_of)
    return jnp.where(strong, factor * drawn, drawn)


def steps_of(own_key, extent, pieces, smallest, largest):
    loudness = 1.0
    for position, blocks in pieces:
        draws = jax.random.uniform(jax.random.fold_in(jax.random.fold_in(own_key, 6), position), (blocks,), jnp.float32, smallest / len(pieces), largest / len(pieces))
        loudness = loudness * jnp.repeat(jnp.exp(draws), extent[position] // blocks).reshape((-1,) + (1,) * (len(extent) - 1 - position))
    return loudness


def noise(key, dims, width, bound, pieces=(), kind=jnp.bfloat16):
    result = width * jax.random.normal(key, dims, jnp.float32)
    if pieces:
        result = result * steps_of(key, dims, pieces, -0.22, 0.18)
    return jnp.clip(result, -bound, bound).astype(kind)


def heavy_noise(own_key, extent, spread, bound, cuts, heavy, kind=jnp.bfloat16):
    result = spread * jax.random.normal(own_key, extent, jnp.float32)
    if cuts:
        result = result * steps_of(own_key, extent, cuts, -0.22, 0.18)
    return jnp.clip(strengthened(result, jax.random.fold_in(own_key, 3), *heavy), -bound, bound).astype(kind)


def setup_inputs(seed: int = 0, part: int = 0) -> dict:
    seeds = jax.random.split(jax.random.key(seed), 11)
    part_keys = jax.random.split(jax.random.fold_in(seeds[10], part), 11)
    return {
        "queries": draw_queries(jax.random.fold_in(jax.random.fold_in(seeds[10], part), 71), part),
        "query_tangent": noise(part_keys[1], (TOKENS, HQ), 1.0, 6.0, ((0, 32), (1, 8))),
        "key_rows": draw_key_rows(jax.random.fold_in(jax.random.fold_in(seeds[10], part), 71), part),
        "key_tangent": noise(part_keys[3], (TOKENS, HQ), 1.0, 6.0, ((0, 32), (1, 8))),
        "value_rows": noise(part_keys[4], (TOKENS, HQ), 1.0, 6.0, ((0, 32), (1, 8))),
        "value_tangent": noise(part_keys[5], (TOKENS, HQ), 1.0, 6.0, ((0, 32), (1, 8))),
        "out_weight": heavy_noise(seeds[6], (HQ, D), HQ ** -0.5, 0.15625, ((0, 8),), (0, 1, 8, 2.0)),
        "out_bias": noise(seeds[7], (D,), 0.5, 3.0, ((0, 8),), jnp.float32),
        "gate_scale": jnp.clip(1.0 + 0.18 * jax.random.normal(part_keys[8], (D,), jnp.float32), 0.1, 1.9),
        "gate_tangent": noise(part_keys[9], (D,), 1.0, 6.0, ((0, 8),), jnp.float32),
    }


def one_head(parts):
    query, query_dot, keys, key_dot, values, value_dot = parts
    factor = HD ** -0.5
    scores = jnp.dot(query, keys.T, preferred_element_type=jnp.float32) * factor
    tilt = (jnp.dot(query_dot, keys.T, preferred_element_type=jnp.float32)
            + jnp.dot(query, key_dot.T, preferred_element_type=jnp.float32)) * factor
    weights = jnp.exp(scores - jnp.max(scores, axis=1, keepdims=True))
    slanted = weights * tilt
    total = jnp.sum(weights, axis=1)
    slope = jnp.sum(slanted, axis=1)
    rounded = weights.astype(jnp.bfloat16)
    tilted = slanted.astype(jnp.bfloat16)
    main = jnp.dot(rounded, values, preferred_element_type=jnp.float32)
    value_part = jnp.dot(rounded, value_dot, preferred_element_type=jnp.float32)
    slope_part = jnp.dot(tilted, values, preferred_element_type=jnp.float32)
    attn = main / total[:, None]
    attn_tangent = (slope_part + value_part) / total[:, None] - attn * (slope / total)[:, None]
    return attn.astype(jnp.bfloat16), attn_tangent.astype(jnp.bfloat16)


def by_head(array):
    return jnp.transpose(array.reshape(TOKENS, HEADS, HD), (1, 0, 2))


def reference(queries, query_tangent, key_rows, key_tangent, value_rows, value_tangent,
              out_weight, out_bias, gate_scale, gate_tangent):
    parts = (by_head(queries), by_head(query_tangent), by_head(key_rows),
             by_head(key_tangent), by_head(value_rows), by_head(value_tangent))
    attn_heads, tangent_heads = lax.map(one_head, parts)
    attn = jnp.transpose(attn_heads, (1, 0, 2)).reshape(TOKENS, HQ)
    attn_tangent = jnp.transpose(tangent_heads, (1, 0, 2)).reshape(TOKENS, HQ)
    group = HQ // N_TP
    proj = jnp.zeros((TOKENS, D), jnp.float32)
    proj_tangent = jnp.zeros((TOKENS, D), jnp.float32)
    for index in range(N_TP):
        lower = index * group
        weight_rows = out_weight[lower:lower + group]
        partial_value = jnp.dot(attn[:, lower:lower + group], weight_rows,
                          preferred_element_type=jnp.float32).astype(jnp.bfloat16)
        partial_tangent = jnp.dot(attn_tangent[:, lower:lower + group], weight_rows,
                                  preferred_element_type=jnp.float32).astype(jnp.bfloat16)
        partial_value, partial_tangent = lax.optimization_barrier((partial_value, partial_tangent))
        proj = proj + partial_value.astype(jnp.float32)
        proj_tangent = proj_tangent + partial_tangent.astype(jnp.float32)
    shifted = proj + out_bias[None, :]
    block_output = (gate_scale[None, :] * shifted).astype(jnp.bfloat16)
    output_tangent = (gate_tangent[None, :] * shifted + gate_scale[None, :] * proj_tangent).astype(jnp.bfloat16)
    return (block_output, output_tangent)
```

```python
import math

import jax
import jax.numpy as jnp
from jax import lax
from jax.experimental import pallas as pl
from jax.experimental.pallas import tpu as pltpu
from jax.sharding import PartitionSpec as P

HD = 128
HEADS = 3
ROWS = 128
HALF = ROWS // 2
RING = 16
STEPS = RING // 2
TP = 8
COLS = 640
FACTOR = HD ** (-0.5)
EXP_SCALE = FACTOR * math.log2(math.e)
MESH = pl.DeviceIdType.MESH
F32 = jnp.float32
BF16 = jnp.bfloat16


def dot_nt(a, b):
    return lax.dot_general(a, b, (((1,), (1,)), ((), ())), preferred_element_type=F32)


def kernel(
    q_ref, qt_ref, k_ref, kt_ref, v_ref, vt_ref, w_ref, bias_ref, scale_ref, slope_ref,
    out_ref, outt_ref,
    kv, qbuf, wbuf, att, proj, top, tot, slp, acc, acct,
    own_part, own_stat, part_out, part_in, stat_out, stat_in,
    ring_send, ring_recv, q_send, q_recv, w_send, w_recv, w_own,
    part_ssem, part_rsem, stat_ssem, stat_rsem, att_send, att_recv,
):
    ctx = lax.axis_index("ctx")
    tp = lax.axis_index("tp")
    z, y = ctx // 2, ctx % 2
    right = lax.rem(z + 1, RING) * 2 + y
    left = lax.rem(z + RING - 1, RING) * 2 + y
    partner = z * 2 + (1 - y)
    peers = [lax.rem(tp + i, TP) for i in range(1, TP)]

    barrier = pltpu.get_barrier_semaphore()
    for where in [{"ctx": right}, {"ctx": left}, {"ctx": partner}] + [{"tp": p} for p in peers]:
        pl.semaphore_signal(barrier, inc=1, device_id=where, device_id_type=MESH)

    for h in range(HEADS):
        cols = slice(h * HD, (h + 1) * HD)
        for i, ref in enumerate((k_ref, kt_ref, v_ref, vt_ref)):
            kv[h, 0, 0:ROWS, i * HD:(i + 1) * HD] = ref[:, cols]
        qbuf[h, 0:ROWS, 0:HD] = qt_ref[:, cols]
        qbuf[h, 0:ROWS, HD:2 * HD] = q_ref[:, cols]

    def ring(h, s, d, c):
        lo = c * HALF
        if isinstance(s, int) and s == STEPS:
            src = kv.at[h, STEPS - 1, pl.ds(d * ROWS + lo, HALF)]
            dst = kv.at[h, 0, pl.ds(ROWS + lo, HALF)]
        else:
            first = isinstance(s, int) and s == 1
            src = kv.at[h, s - 1, pl.ds((0 if first else d * ROWS) + lo, HALF)]
            dst = kv.at[h, s, pl.ds(d * ROWS + lo, HALF)]
        return pltpu.make_async_remote_copy(
            src_ref=src, dst_ref=dst,
            send_sem=ring_send.at[h, s - 1, d, c], recv_sem=ring_recv.at[h, s - 1, d, c],
            device_id={"ctx": right if d == 0 else left}, device_id_type=MESH)

    def start_ring(h):
        for c in range(2):
            for d in range(2):
                ring(h, 1, d, c).start()

    def q_copy(h):
        return pltpu.make_async_remote_copy(
            src_ref=qbuf.at[h, pl.ds(0, ROWS)], dst_ref=qbuf.at[h, pl.ds(ROWS, ROWS)],
            send_sem=q_send.at[h], recv_sem=q_recv.at[h],
            device_id={"ctx": partner}, device_id_type=MESH)

    def w_copy(i):
        peer = lax.rem(tp + i + 1, TP)
        return pltpu.make_async_remote_copy(
            src_ref=w_ref.at[:, :, pl.ds(pl.multiple_of(peer * COLS, COLS), COLS)],
            dst_ref=wbuf.at[:, pl.ds(pl.multiple_of(tp * HD, HD), HD), :],
            send_sem=w_send.at[i], recv_sem=w_recv.at[i],
            device_id={"tp": peer}, device_id_type=MESH)

    def att_copy(h, i):
        peer = lax.rem(tp + i + 1, TP)
        mine = att.at[h, :, pl.ds(pl.multiple_of(tp * HD, HD), HD)]
        return pltpu.make_async_remote_copy(
            src_ref=mine, dst_ref=mine,
            send_sem=att_send.at[h, i], recv_sem=att_recv.at[h, i],
            device_id={"tp": peer}, device_id_type=MESH)

    def part_copy(h):
        return pltpu.make_async_remote_copy(
            src_ref=part_out.at[h], dst_ref=part_in.at[h],
            send_sem=part_ssem.at[h], recv_sem=part_rsem.at[h],
            device_id={"ctx": partner}, device_id_type=MESH)

    def stat_copy(h):
        return pltpu.make_async_remote_copy(
            src_ref=stat_out.at[h], dst_ref=stat_in.at[h],
            send_sem=stat_ssem.at[h], recv_sem=stat_rsem.at[h],
            device_id={"ctx": partner}, device_id_type=MESH)

    own_w = pltpu.make_async_copy(
        w_ref.at[:, :, pl.ds(pl.multiple_of(tp * COLS, COLS), COLS)],
        wbuf.at[:, pl.ds(pl.multiple_of(tp * HD, HD), HD), :], w_own)

    pl.semaphore_wait(barrier, 3 + TP - 1)
    start_ring(0)
    for h in range(HEADS):
        q_copy(h).start()
    for i in range(TP - 1):
        w_copy(i).start()
    own_w.start()

    def attend(h, block, first=False):
        pair = qbuf[h]
        keys = block[:, 0:2 * HD]
        scores = dot_nt(pair[:, HD:], keys[:, :HD])
        tilt = dot_nt(pair, keys)
        count = scores.shape[1]
        peak = jnp.max(scores, axis=1, keepdims=True)
        if first:
            new = jnp.broadcast_to(peak, (2 * ROWS, HD))
        else:
            old = top[...]
            new = jnp.maximum(old, peak)
            shrink = jnp.exp2((old - new) * EXP_SCALE)
        top[...] = new
        wide = jnp.concatenate([new] * (count // HD), axis=1) if count > HD else new
        weights = jnp.exp2((scores - wide) * EXP_SCALE)
        slanted = weights * tilt
        folded, tilted = weights[:, :HD], slanted[:, :HD]
        for i in range(1, count // HD):
            folded = folded + weights[:, i * HD:(i + 1) * HD]
            tilted = tilted + slanted[:, i * HD:(i + 1) * HD]
        values = block[:, 2 * HD:]
        both = jnp.dot(weights.astype(BF16), values, preferred_element_type=F32)
        bent = jnp.dot(slanted.astype(BF16), values[:, :HD], preferred_element_type=F32)
        if first:
            tot[...] = folded
            slp[...] = tilted
            acc[...] = both
            acct[...] = bent
        else:
            tot[...] = tot[...] * shrink + folded
            slp[...] = slp[...] * shrink + tilted
            acc[...] = acc[...] * jnp.concatenate([shrink, shrink], axis=1) + both
            acct[...] = acct[...] * shrink + bent

    def part_of(h):
        total = jnp.sum(tot[...], axis=1, keepdims=True)
        incline = jnp.sum(slp[...], axis=1, keepdims=True) * FACTOR
        inverse = 1.0 / total
        incline = incline * inverse
        main = acc[:, :HD] * inverse
        tangent = (acct[...] * FACTOR + acc[:, HD:]) * inverse - main * incline
        own_part[h, :, :HD] = main[:ROWS]
        own_part[h, :, HD:] = tangent[:ROWS]
        part_out[h, :, :HD] = main[ROWS:].astype(BF16)
        part_out[h, :, HD:] = tangent[ROWS:].astype(BF16)
        part_copy(h).start()
        lane = lax.broadcasted_iota(jnp.int32, (ROWS, HD), 1)
        stat = jnp.where(lane == 0, top[ROWS:, :], jnp.where(lane == 1, total[ROWS:], incline[ROWS:]))
        stat_out[h] = stat.T[0:8]
        stat_copy(h).start()
        own_stat[h, 0] = top[0:ROWS, :]
        own_stat[h, 1] = jnp.broadcast_to(total[:ROWS], (ROWS, HD))
        own_stat[h, 2] = jnp.broadcast_to(incline[:ROWS], (ROWS, HD))

    def join(h):
        stat_copy(h).wait_recv()
        part_copy(h).wait_recv()
        theirs = jnp.concatenate([stat_in[h]] * (HD // 8), axis=0).T
        top1, total1, incline1 = theirs[:, 0:1], theirs[:, 1:2], theirs[:, 2:3]
        top0, total0, incline0 = own_stat[h, 0], own_stat[h, 1], own_stat[h, 2]
        high = jnp.maximum(top0, top1)
        share0 = total0 * jnp.exp2((top0 - high) * EXP_SCALE)
        share1 = total1 * jnp.exp2((top1 - high) * EXP_SCALE)
        inverse = 1.0 / (share0 + share1)
        share0 = share0 * inverse
        share1 = share1 * inverse
        incline = share0 * incline0 + share1 * incline1
        main0, tan0 = own_part[h, :, :HD], own_part[h, :, HD:]
        main1, tan1 = part_in[h, :, :HD].astype(F32), part_in[h, :, HD:].astype(F32)
        main = share0 * main0 + share1 * main1
        tangent = (share0 * (tan0 + main0 * (incline0 - incline))
                   + share1 * (tan1 + main1 * (incline1 - incline)))
        cols = pl.ds(pl.multiple_of(tp * HD, HD), HD)
        att[h, 0:ROWS, cols] = main.astype(BF16)
        att[h, ROWS:2 * ROWS, cols] = tangent.astype(BF16)
        for i in range(TP - 1):
            att_copy(h, i).start()

    def project(h):
        for i in range(TP - 1):
            att_copy(h, i).wait_recv()
        if h == 0:
            own_w.wait()
            for i in range(TP - 1):
                w_copy(i).wait_recv()
        term = jnp.dot(att[h], wbuf[h], preferred_element_type=F32)
        if h == 0:
            proj[...] = term
        else:
            proj[...] += term

    def pass_on(h, s, sends=((0, 0), (0, 1), (1, 0), (1, 1))):
        for c in range(2):
            for d in range(2):
                ring(h, s, d, c).wait_recv()
                if (c, d) in sends:
                    ring(h, s + 1, d, c).start()

    for h in range(HEADS):
        if h == 0:
            pass_on(0, 1)
            pass_on(0, 2)
            for i in range(HEADS):
                q_copy(i).wait_recv()
            attend(0, kv.at[0, 0, pl.ds(0, ROWS)], first=True)
            attend(0, kv.at[0, 1])
            attend(0, kv.at[0, 2])
            begin = 3
        else:
            attend(h, kv.at[h, 0, pl.ds(0, ROWS)], first=True)
            begin = 1

        def turn(s, carry, h=h):
            pass_on(h, s)
            attend(h, kv.at[h, s])
            return carry

        if begin == 1:
            pass_on(h, 1)
            attend(h, kv.at[h, 1])
            begin = 2
        lax.fori_loop(begin, 4, turn, 0)
        if h > 0:
            join(h - 1)
        lax.fori_loop(4, STEPS - 1, turn, 0)
        pass_on(h, STEPS - 1, sends=((0, 0), (1, 1)))
        if h + 1 < HEADS:
            start_ring(h + 1)
        attend(h, kv.at[h, STEPS - 1])
        ring(h, STEPS, 0, 0).wait_recv()
        ring(h, STEPS, 1, 1).wait_recv()
        attend(h, kv.at[h, 0, pl.ds(ROWS, ROWS)])
        part_of(h)

    project(0)
    project(1)
    join(HEADS - 1)
    project(HEADS - 1)

    shifted = proj[0:ROWS, :] + bias_ref[...]
    out_ref[...] = (scale_ref[...] * shifted).astype(BF16)
    outt_ref[...] = (slope_ref[...] * shifted + scale_ref[...] * proj[ROWS:2 * ROWS, :]).astype(BF16)

    for h in range(HEADS):
        q_copy(h).wait_send()
        part_copy(h).wait_send()
        stat_copy(h).wait_send()
        for i in range(TP - 1):
            att_copy(h, i).wait_send()
        for s in range(1, STEPS):
            for c in range(2):
                for d in range(2):
                    ring(h, s, d, c).wait_send()
        ring(h, STEPS, 0, 0).wait_send()
        ring(h, STEPS, 1, 1).wait_send()
    for i in range(TP - 1):
        w_copy(i).wait_send()


def per_device(q, qt, k, kt, v, vt, w, bias, scale, slope):
    vm = pl.BlockSpec(memory_space=pltpu.VMEM)
    dma = pltpu.SemaphoreType.DMA
    shape = jax.ShapeDtypeStruct((ROWS, COLS), BF16)
    return pl.pallas_call(
        kernel,
        out_shape=(shape, shape),
        in_specs=[vm] * 6 + [pl.BlockSpec(memory_space=pl.ANY)] + [vm] * 3,
        out_specs=(vm, vm),
        scratch_shapes=[
            pltpu.VMEM((HEADS, STEPS, 2 * ROWS, 4 * HD), BF16),
            pltpu.VMEM((HEADS, 2 * ROWS, 2 * HD), BF16),
            pltpu.VMEM((HEADS, TP * HD, COLS), BF16),
            pltpu.VMEM((HEADS, 2 * ROWS, TP * HD), BF16),
            pltpu.VMEM((2 * ROWS, COLS), F32),
            pltpu.VMEM((2 * ROWS, HD), F32),
            pltpu.VMEM((2 * ROWS, HD), F32),
            pltpu.VMEM((2 * ROWS, HD), F32),
            pltpu.VMEM((2 * ROWS, 2 * HD), F32),
            pltpu.VMEM((2 * ROWS, HD), F32),
            pltpu.VMEM((HEADS, ROWS, 2 * HD), F32),
            pltpu.VMEM((HEADS, 3, ROWS, HD), F32),
            pltpu.VMEM((HEADS, ROWS, 2 * HD), BF16),
            pltpu.VMEM((HEADS, ROWS, 2 * HD), BF16),
            pltpu.VMEM((HEADS, 8, HD), F32),
            pltpu.VMEM((HEADS, 8, HD), F32),
            dma((HEADS, STEPS, 2, 2)), dma((HEADS, STEPS, 2, 2)),
            dma((HEADS,)), dma((HEADS,)),
            dma((TP - 1,)), dma((TP - 1,)), dma,
            dma((HEADS,)), dma((HEADS,)), dma((HEADS,)), dma((HEADS,)),
            dma((HEADS, TP - 1)), dma((HEADS, TP - 1)),
        ],
        compiler_params=pltpu.CompilerParams(
            collective_id=0, has_side_effects=True, vmem_limit_bytes=48 * 2**20),
        name="attention",
    )(q, qt, k, kt, v, vt, w.reshape(HEADS, HD, -1), bias.reshape(1, -1),
      scale.reshape(1, -1), slope.reshape(1, -1))


def solution(mesh):
    in_specs = (
        P(("dp", "ctx"), "tp"),
        P(("dp", "ctx"), "tp"),
        P(("dp", "ctx"), "tp"),
        P(("dp", "ctx"), "tp"),
        P(("dp", "ctx"), "tp"),
        P(("dp", "ctx"), "tp"),
        P("tp", None),
        P("tp"),
        P(("dp", "tp")),
        P(("dp", "tp")),
    )
    out_specs = (P(("dp", "ctx"), "tp"), P(("dp", "ctx"), "tp"))
    return jax.shard_map(
        per_device, mesh=mesh, in_specs=in_specs, out_specs=out_specs, check_vma=False
    )
```

```python
import math

import jax
import jax.numpy as jnp
from jax import lax
from jax.experimental import pallas as pl
from jax.experimental.pallas import tpu as pltpu
from jax.sharding import PartitionSpec as P

HD = 128
HEADS = 3
ROWS = 128
HALF = ROWS // 2
RING = 16
STEPS = RING // 2
LAG = 2
TP = 8
COLS = 640
FACTOR = HD ** (-0.5)
EXP_SCALE = FACTOR * math.log2(math.e)
MESH = pl.DeviceIdType.MESH
F32 = jnp.float32
BF16 = jnp.bfloat16


def dot_nt(a, b):
    return lax.dot_general(a, b, (((1,), (1,)), ((), ())), preferred_element_type=F32)


def kernel(
    q_ref, qt_ref, k_ref, kt_ref, v_ref, vt_ref, w_ref, bias_ref, scale_ref, slope_ref,
    out_ref, outt_ref,
    bias, scale, slope, kv, qbuf, wbuf, att, proj, top, tot, slp, acc, acct,
    own_part, own_stat, part_out, part_in, stat_out, stat_in,
    ring_send, ring_recv, q_send, q_recv, w_send, w_recv, w_own,
    part_ssem, part_rsem, stat_ssem, stat_rsem, att_send, att_recv, load_sem, gate_sem,
):
    ctx = lax.axis_index("ctx")
    tp = lax.axis_index("tp")
    z, y = ctx // 2, ctx % 2
    right = lax.rem(z + 1, RING) * 2 + y
    left = lax.rem(z + RING - 1, RING) * 2 + y
    partner = z * 2 + (1 - y)
    peers = [lax.rem(tp + i, TP) for i in range(1, TP)]

    barrier = pltpu.get_barrier_semaphore()
    for where in [{"ctx": right}, {"ctx": left}, {"ctx": partner}] + [{"tp": p} for p in peers]:
        pl.semaphore_signal(barrier, inc=1, device_id=where, device_id_type=MESH)

    def load_copies(h):
        cols = pl.ds(h * HD, HD)
        targets = [(ref, kv.at[h, 0, pl.ds(0, ROWS), pl.ds(i * HD, HD)])
                   for i, ref in enumerate((k_ref, kt_ref, v_ref, vt_ref))]
        targets += [(ref, qbuf.at[h, pl.ds(0, ROWS), pl.ds(i * HD, HD)])
                    for i, ref in enumerate((qt_ref, q_ref))]
        return [pltpu.make_async_copy(ref.at[:, cols], target, load_sem.at[h, i])
                for i, (ref, target) in enumerate(targets)]

    gate_copies = [pltpu.make_async_copy(ref, target, gate_sem.at[i])
                   for i, (ref, target) in enumerate(
                       ((bias_ref, bias), (scale_ref, scale), (slope_ref, slope)))]
    for h in range(HEADS):
        for copy in load_copies(h):
            copy.start()
    for copy in gate_copies:
        copy.start()

    def ring(h, s, d, c):
        lo = c * HALF
        if isinstance(s, int) and s == STEPS:
            src = kv.at[h, STEPS - 1, pl.ds(d * ROWS + lo, HALF)]
            dst = kv.at[h, 0, pl.ds(ROWS + lo, HALF)]
        else:
            first = isinstance(s, int) and s == 1
            src = kv.at[h, s - 1, pl.ds((0 if first else d * ROWS) + lo, HALF)]
            dst = kv.at[h, s, pl.ds(d * ROWS + lo, HALF)]
        return pltpu.make_async_remote_copy(
            src_ref=src, dst_ref=dst,
            send_sem=ring_send.at[h, s - 1, d, c], recv_sem=ring_recv.at[h, s - 1, d, c],
            device_id={"ctx": right if d == 0 else left}, device_id_type=MESH)

    def start_ring(h):
        for c in range(2):
            for d in range(2):
                ring(h, 1, d, c).start()

    def q_copy(h):
        return pltpu.make_async_remote_copy(
            src_ref=qbuf.at[h, pl.ds(0, ROWS)], dst_ref=qbuf.at[h, pl.ds(ROWS, ROWS)],
            send_sem=q_send.at[h], recv_sem=q_recv.at[h],
            device_id={"ctx": partner}, device_id_type=MESH)

    def w_copy(i):
        peer = lax.rem(tp + i + 1, TP)
        return pltpu.make_async_remote_copy(
            src_ref=w_ref.at[:, :, pl.ds(pl.multiple_of(peer * COLS, COLS), COLS)],
            dst_ref=wbuf.at[:, pl.ds(pl.multiple_of(tp * HD, HD), HD), :],
            send_sem=w_send.at[i], recv_sem=w_recv.at[i],
            device_id={"tp": peer}, device_id_type=MESH)

    def att_copy(h, i):
        peer = lax.rem(tp + i + 1, TP)
        mine = att.at[h, :, pl.ds(pl.multiple_of(tp * HD, HD), HD)]
        return pltpu.make_async_remote_copy(
            src_ref=mine, dst_ref=mine,
            send_sem=att_send.at[h, i], recv_sem=att_recv.at[h, i],
            device_id={"tp": peer}, device_id_type=MESH)

    def part_copy(h):
        return pltpu.make_async_remote_copy(
            src_ref=part_out.at[h], dst_ref=part_in.at[h],
            send_sem=part_ssem.at[h], recv_sem=part_rsem.at[h],
            device_id={"ctx": partner}, device_id_type=MESH)

    def stat_copy(h):
        return pltpu.make_async_remote_copy(
            src_ref=stat_out.at[h], dst_ref=stat_in.at[h],
            send_sem=stat_ssem.at[h], recv_sem=stat_rsem.at[h],
            device_id={"ctx": partner}, device_id_type=MESH)

    own_w = pltpu.make_async_copy(
        w_ref.at[:, :, pl.ds(pl.multiple_of(tp * COLS, COLS), COLS)],
        wbuf.at[:, pl.ds(pl.multiple_of(tp * HD, HD), HD), :], w_own)

    pl.semaphore_wait(barrier, 3 + TP - 1)
    for h in range(HEADS):
        for copy in load_copies(h):
            copy.wait()
        if h == 0:
            start_ring(0)
        q_copy(h).start()
    for i in range(TP - 1):
        w_copy(i).start()
    own_w.start()

    def attend(h, block, first=False):
        pair = qbuf[h]
        keys = block[:, 0:2 * HD]
        scores = dot_nt(pair[:, HD:], keys[:, :HD])
        tilt = dot_nt(pair, keys)
        count = scores.shape[1]
        peak = jnp.max(scores, axis=1, keepdims=True)
        if first:
            new = jnp.broadcast_to(peak, (2 * ROWS, HD))
        else:
            old = top[h]
            new = jnp.maximum(old, peak)
            shrink = jnp.exp2((old - new) * EXP_SCALE)
        top[h] = new
        wide = jnp.concatenate([new] * (count // HD), axis=1) if count > HD else new
        weights = jnp.exp2((scores - wide) * EXP_SCALE)
        slanted = weights * tilt
        folded, tilted = weights[:, :HD], slanted[:, :HD]
        for i in range(1, count // HD):
            folded = folded + weights[:, i * HD:(i + 1) * HD]
            tilted = tilted + slanted[:, i * HD:(i + 1) * HD]
        values = block[:, 2 * HD:]
        both = jnp.dot(weights.astype(BF16), values, preferred_element_type=F32)
        bent = jnp.dot(slanted.astype(BF16), values[:, :HD], preferred_element_type=F32)
        if first:
            tot[h] = folded
            slp[h] = tilted
            acc[h] = both
            acct[h] = bent
        else:
            tot[h] = tot[h] * shrink + folded
            slp[h] = slp[h] * shrink + tilted
            acc[h] = acc[h] * jnp.concatenate([shrink, shrink], axis=1) + both
            acct[h] = acct[h] * shrink + bent

    def part_of(h):
        total = jnp.sum(tot[h], axis=1, keepdims=True)
        incline = jnp.sum(slp[h], axis=1, keepdims=True) * FACTOR
        inverse = 1.0 / total
        incline = incline * inverse
        main = acc[h, :, :HD] * inverse
        tangent = (acct[h] * FACTOR + acc[h, :, HD:]) * inverse - main * incline
        own_part[h, :, :HD] = main[:ROWS]
        own_part[h, :, HD:] = tangent[:ROWS]
        part_out[h, :, :HD] = main[ROWS:].astype(BF16)
        part_out[h, :, HD:] = tangent[ROWS:].astype(BF16)
        part_copy(h).start()
        lane = lax.broadcasted_iota(jnp.int32, (ROWS, HD), 1)
        stat = jnp.where(lane == 0, top[h, ROWS:, :], jnp.where(lane == 1, total[ROWS:], incline[ROWS:]))
        stat_out[h] = stat.T[0:8]
        stat_copy(h).start()
        own_stat[h, 0] = top[h, 0:ROWS, :]
        own_stat[h, 1] = jnp.broadcast_to(total[:ROWS], (ROWS, HD))
        own_stat[h, 2] = jnp.broadcast_to(incline[:ROWS], (ROWS, HD))

    def join(h):
        stat_copy(h).wait_recv()
        part_copy(h).wait_recv()
        theirs = jnp.concatenate([stat_in[h]] * (HD // 8), axis=0).T
        top1, total1, incline1 = theirs[:, 0:1], theirs[:, 1:2], theirs[:, 2:3]
        top0, total0, incline0 = own_stat[h, 0], own_stat[h, 1], own_stat[h, 2]
        high = jnp.maximum(top0, top1)
        share0 = total0 * jnp.exp2((top0 - high) * EXP_SCALE)
        share1 = total1 * jnp.exp2((top1 - high) * EXP_SCALE)
        inverse = 1.0 / (share0 + share1)
        share0 = share0 * inverse
        share1 = share1 * inverse
        incline = share0 * incline0 + share1 * incline1
        main0, tan0 = own_part[h, :, :HD], own_part[h, :, HD:]
        main1, tan1 = part_in[h, :, :HD].astype(F32), part_in[h, :, HD:].astype(F32)
        main = share0 * main0 + share1 * main1
        tangent = (share0 * (tan0 + main0 * (incline0 - incline))
                   + share1 * (tan1 + main1 * (incline1 - incline)))
        cols = pl.ds(pl.multiple_of(tp * HD, HD), HD)
        att[h, 0:ROWS, cols] = main.astype(BF16)
        att[h, ROWS:2 * ROWS, cols] = tangent.astype(BF16)
        for i in range(TP - 1):
            att_copy(h, i).start()

    def project(h):
        for i in range(TP - 1):
            att_copy(h, i).wait_recv()
        if h == 0:
            own_w.wait()
            for i in range(TP - 1):
                w_copy(i).wait_recv()
        term = jnp.dot(att[h], wbuf[h], preferred_element_type=F32)
        if h == 0:
            proj[...] = term
        else:
            proj[...] += term

    def pass_on(h, s, sends=((0, 0), (0, 1), (1, 0), (1, 1))):
        for c in range(2):
            for d in range(2):
                ring(h, s, d, c).wait_recv()
                if (c, d) in sends:
                    ring(h, s + 1, d, c).start()

    def slot(k, attending):
        def at(h):
            return k - h * LAG

        if not isinstance(k, int):
            for h in range(1, HEADS - 1):
                pl.when(k == STEPS + (h + 1) * LAG)(lambda h=h: join(h))
        for h in range(HEADS):
            s = at(h)
            if isinstance(k, int):
                if 1 <= s < STEPS - 1:
                    pass_on(h, s)
            else:
                pl.when((s >= 2) & (s < STEPS - 1))(lambda h=h, s=s: pass_on(h, s))
                pl.when(s == 1)(lambda h=h: pass_on(h, 1))
                pl.when(s == STEPS - 1)(lambda h=h: pass_on(h, STEPS - 1, ((0, 0), (1, 1))))
            if h > 0:
                if isinstance(k, int):
                    if s == 0:
                        start_ring(h)
                else:
                    pl.when(s == 0)(lambda h=h: start_ring(h))
        if not attending:
            return
        for h in range(HEADS):
            s = at(h)

            def inner(h=h, s=s):
                pl.when(s == 1)(lambda: attend(h, kv.at[h, 0, pl.ds(0, ROWS)], first=True))
                attend(h, kv.at[h, s])

            def last(h=h):
                ring(h, STEPS, 0, 0).wait_recv()
                ring(h, STEPS, 1, 1).wait_recv()
                attend(h, kv.at[h, 0, pl.ds(ROWS, ROWS)])
                part_of(h)

            pl.when((s >= 1) & (s < STEPS))(inner)
            pl.when(s == STEPS)(last)
        pl.when(k == STEPS + LAG)(lambda: join(0))

    for k in range(1, 3):
        slot(k, False)
    for i in range(HEADS):
        q_copy(i).wait_recv()
    for h in range(HEADS):
        if 2 - h * LAG >= 1:
            attend(h, kv.at[h, 0, pl.ds(0, ROWS)], first=True)
        for s in range(1, 3 - h * LAG):
            attend(h, kv.at[h, s])

    def turn(k, carry):
        slot(k, True)
        return carry

    lax.fori_loop(3, STEPS + (HEADS - 1) * LAG + 1, turn, 0)

    project(0)
    project(1)
    join(HEADS - 1)
    project(HEADS - 1)

    for copy in gate_copies:
        copy.wait()
    gate, gate_dot = scale[...].reshape(1, COLS), slope[...].reshape(1, COLS)
    shifted = proj[0:ROWS, :] + bias[...].reshape(1, COLS)
    out_ref[...] = (gate * shifted).astype(BF16)
    outt_ref[...] = (gate_dot * shifted + gate * proj[ROWS:2 * ROWS, :]).astype(BF16)

    for h in range(HEADS):
        q_copy(h).wait_send()
        part_copy(h).wait_send()
        stat_copy(h).wait_send()
        for i in range(TP - 1):
            att_copy(h, i).wait_send()
        for s in range(1, STEPS):
            for c in range(2):
                for d in range(2):
                    ring(h, s, d, c).wait_send()
        ring(h, STEPS, 0, 0).wait_send()
        ring(h, STEPS, 1, 1).wait_send()
    for i in range(TP - 1):
        w_copy(i).wait_send()


def per_device(q, qt, k, kt, v, vt, w, bias, scale, slope):
    vm = pl.BlockSpec(memory_space=pltpu.VMEM)
    dma = pltpu.SemaphoreType.DMA
    shape = jax.ShapeDtypeStruct((ROWS, COLS), BF16)
    return pl.pallas_call(
        kernel,
        out_shape=(shape, shape),
        in_specs=[pl.BlockSpec(memory_space=pl.ANY)] * 10,
        out_specs=(vm, vm),
        scratch_shapes=[
            pltpu.VMEM((COLS,), F32), pltpu.VMEM((COLS,), F32), pltpu.VMEM((COLS,), F32),
            pltpu.VMEM((HEADS, STEPS, 2 * ROWS, 4 * HD), BF16),
            pltpu.VMEM((HEADS, 2 * ROWS, 2 * HD), BF16),
            pltpu.VMEM((HEADS, TP * HD, COLS), BF16),
            pltpu.VMEM((HEADS, 2 * ROWS, TP * HD), BF16),
            pltpu.VMEM((2 * ROWS, COLS), F32),
            pltpu.VMEM((HEADS, 2 * ROWS, HD), F32),
            pltpu.VMEM((HEADS, 2 * ROWS, HD), F32),
            pltpu.VMEM((HEADS, 2 * ROWS, HD), F32),
            pltpu.VMEM((HEADS, 2 * ROWS, 2 * HD), F32),
            pltpu.VMEM((HEADS, 2 * ROWS, HD), F32),
            pltpu.VMEM((HEADS, ROWS, 2 * HD), F32),
            pltpu.VMEM((HEADS, 3, ROWS, HD), F32),
            pltpu.VMEM((HEADS, ROWS, 2 * HD), BF16),
            pltpu.VMEM((HEADS, ROWS, 2 * HD), BF16),
            pltpu.VMEM((HEADS, 8, HD), F32),
            pltpu.VMEM((HEADS, 8, HD), F32),
            dma((HEADS, STEPS, 2, 2)), dma((HEADS, STEPS, 2, 2)),
            dma((HEADS,)), dma((HEADS,)),
            dma((TP - 1,)), dma((TP - 1,)), dma,
            dma((HEADS,)), dma((HEADS,)), dma((HEADS,)), dma((HEADS,)),
            dma((HEADS, TP - 1)), dma((HEADS, TP - 1)), dma((HEADS, 6)), dma((3,)),
        ],
        compiler_params=pltpu.CompilerParams(
            collective_id=0, has_side_effects=True, vmem_limit_bytes=63 * 2**20),
        name="attention",
    )(q, qt, k, kt, v, vt, w.reshape(HEADS, HD, -1), bias, scale, slope)


def solution(mesh):
    in_specs = (
        P(("dp", "ctx"), "tp"),
        P(("dp", "ctx"), "tp"),
        P(("dp", "ctx"), "tp"),
        P(("dp", "ctx"), "tp"),
        P(("dp", "ctx"), "tp"),
        P(("dp", "ctx"), "tp"),
        P("tp", None),
        P("tp"),
        P(("dp", "tp")),
        P(("dp", "tp")),
    )
    out_specs = (P(("dp", "ctx"), "tp"), P(("dp", "ctx"), "tp"))
    return jax.shard_map(
        per_device, mesh=mesh, in_specs=in_specs, out_specs=out_specs, check_vma=False
    )
```

```python
import math

import jax
import jax.numpy as jnp
from jax import lax
from jax.experimental import pallas as pl
from jax.experimental.pallas import tpu as pltpu
from jax.sharding import PartitionSpec as P

HD = 128
HEADS = 3
ROWS = 128
HALF = ROWS // 2
RING = 16
STEPS = RING // 2
OFFSET = (0, 2, 4)
START = (0, 0, 2)
TP = 8
CHIPS = TP // 2 - 1
COLS = 640
FACTOR = HD ** (-0.5)
EXP_SCALE = FACTOR * math.log2(math.e)
MESH = pl.DeviceIdType.MESH
F32 = jnp.float32
BF16 = jnp.bfloat16


def dot_nt(a, b):
    return lax.dot_general(a, b, (((1,), (1,)), ((), ())), preferred_element_type=F32)


def kernel(
    q_ref, qt_ref, k_ref, kt_ref, v_ref, vt_ref, w_ref, out_ref,
    kv, qbuf, wbuf, att, proj, top, tot, slp, acc, acct,
    own_part, own_stat, part_out, part_in, stat_out, stat_in,
    ring_send, ring_recv, q_send, q_recv, w_send, w_recv, w_own,
    part_ssem, part_rsem, stat_ssem, stat_rsem, att_send, att_recv, load_sem,
):
    ctx = lax.axis_index("ctx")
    tp = lax.axis_index("tp")
    z, y = ctx // 2, ctx % 2
    right = lax.rem(z + 1, RING) * 2 + y
    left = lax.rem(z + RING - 1, RING) * 2 + y
    far_right = lax.rem(z + 2, RING) * 2 + y
    far_left = lax.rem(z + RING - 2, RING) * 2 + y
    partner = z * 2 + (1 - y)
    sibling = tp + 1 - 2 * lax.rem(tp, 2)
    peers = [lax.rem(tp + i, TP) for i in range(1, TP)]

    barrier = pltpu.get_barrier_semaphore()
    for where in [{"ctx": c} for c in (right, left, far_right, far_left, partner)] + [{"tp": p} for p in peers]:
        pl.semaphore_signal(barrier, inc=1, device_id=where, device_id_type=MESH)

    def load_copies(h):
        cols = pl.ds(h * HD, HD)
        targets = [(ref, kv.at[h, 0, pl.ds(0, ROWS), pl.ds(i * HD, HD)])
                   for i, ref in enumerate((k_ref, kt_ref, v_ref, vt_ref))]
        targets += [(ref, qbuf.at[h, pl.ds(0, ROWS), pl.ds(i * HD, HD)])
                    for i, ref in enumerate((qt_ref, q_ref))]
        return [pltpu.make_async_copy(ref.at[:, cols], target, load_sem.at[h, i])
                for i, (ref, target) in enumerate(targets)]

    for h in range(HEADS):
        for copy in load_copies(h):
            copy.start()

    def ring(h, s, d, c):
        lo = c * HALF
        targets = (right, left)
        if isinstance(s, int) and s == STEPS:
            back = 1
            if h == HEADS - 1:
                back, targets = 2, (far_right, far_left)
            src = kv.at[h, STEPS - back, pl.ds(d * ROWS + lo, HALF)]
            dst = kv.at[h, 0, pl.ds(ROWS + lo, HALF)]
        else:
            first = isinstance(s, int) and s == 1
            src = kv.at[h, s - 1, pl.ds((0 if first else d * ROWS) + lo, HALF)]
            dst = kv.at[h, s, pl.ds(d * ROWS + lo, HALF)]
        return pltpu.make_async_remote_copy(
            src_ref=src, dst_ref=dst,
            send_sem=ring_send.at[h, s - 1, d, c], recv_sem=ring_recv.at[h, s - 1, d, c],
            device_id={"ctx": targets[d]}, device_id_type=MESH)

    def start_ring(h):
        for c in range(2):
            for d in range(2):
                ring(h, 1, d, c).start()

    def q_copy(h):
        return pltpu.make_async_remote_copy(
            src_ref=qbuf.at[h, pl.ds(0, ROWS)], dst_ref=qbuf.at[h, pl.ds(ROWS, ROWS)],
            send_sem=q_send.at[h], recv_sem=q_recv.at[h],
            device_id={"ctx": partner}, device_id_type=MESH)

    def w_copy(i):
        peer = lax.rem(tp + i + 1, TP)
        return pltpu.make_async_remote_copy(
            src_ref=w_ref.at[:, :, pl.ds(pl.multiple_of(peer * COLS, COLS), COLS)],
            dst_ref=wbuf.at[:, pl.ds(pl.multiple_of(tp * HD, HD), HD), :],
            send_sem=w_send.at[i], recv_sem=w_recv.at[i],
            device_id={"tp": peer}, device_id_type=MESH)

    def att_copy(h, i):
        owner = tp if i <= CHIPS else lax.rem(tp + TP - 2 * (i - CHIPS), TP)
        peer = lax.rem(tp + 2 * (i + 1), TP) if i < CHIPS else sibling
        part = att.at[h, :, pl.ds(pl.multiple_of(owner * HD, HD), HD)]
        return pltpu.make_async_remote_copy(
            src_ref=part, dst_ref=part,
            send_sem=att_send.at[h, i], recv_sem=att_recv.at[h, i],
            device_id={"tp": peer}, device_id_type=MESH)

    def relay(h):
        for i in range(CHIPS):
            att_copy(h, i).wait_recv()
            att_copy(h, CHIPS + 1 + i).start()

    def part_copy(h):
        return pltpu.make_async_remote_copy(
            src_ref=part_out.at[h], dst_ref=part_in.at[h],
            send_sem=part_ssem.at[h], recv_sem=part_rsem.at[h],
            device_id={"ctx": partner}, device_id_type=MESH)

    def stat_copy(h):
        return pltpu.make_async_remote_copy(
            src_ref=stat_out.at[h], dst_ref=stat_in.at[h],
            send_sem=stat_ssem.at[h], recv_sem=stat_rsem.at[h],
            device_id={"ctx": partner}, device_id_type=MESH)

    own_w = pltpu.make_async_copy(
        w_ref.at[:, :, pl.ds(pl.multiple_of(tp * COLS, COLS), COLS)],
        wbuf.at[:, pl.ds(pl.multiple_of(tp * HD, HD), HD), :], w_own)

    pl.semaphore_wait(barrier, 5 + TP - 1)
    for h in range(HEADS):
        for copy in load_copies(h):
            copy.wait()
        if START[h] == 0:
            start_ring(h)
    for h in range(HEADS):
        q_copy(h).start()
    for i in range(TP - 1):
        w_copy(i).start()
    own_w.start()

    def attend(h, block, first=False):
        pair = qbuf[h]
        keys = block[:, 0:2 * HD]
        scores = dot_nt(pair[:, HD:], keys[:, :HD])
        tilt = dot_nt(pair, keys)
        count = scores.shape[1]
        peak = jnp.max(scores, axis=1, keepdims=True)
        if first:
            new = jnp.broadcast_to(peak, (2 * ROWS, HD))
        else:
            old = top[h]
            new = jnp.maximum(old, peak)
            shrink = jnp.exp2((old - new) * EXP_SCALE)
        top[h] = new
        wide = jnp.concatenate([new] * (count // HD), axis=1) if count > HD else new
        weights = jnp.exp2((scores - wide) * EXP_SCALE)
        slanted = weights * tilt
        folded, tilted = weights[:, :HD], slanted[:, :HD]
        for i in range(1, count // HD):
            folded = folded + weights[:, i * HD:(i + 1) * HD]
            tilted = tilted + slanted[:, i * HD:(i + 1) * HD]
        values = block[:, 2 * HD:]
        both = jnp.dot(weights.astype(BF16), values, preferred_element_type=F32)
        bent = jnp.dot(slanted.astype(BF16), values[:, :HD], preferred_element_type=F32)
        if first:
            tot[h] = folded
            slp[h] = tilted
            acc[h] = both
            acct[h] = bent
        else:
            tot[h] = tot[h] * shrink + folded
            slp[h] = slp[h] * shrink + tilted
            acc[h] = acc[h] * jnp.concatenate([shrink, shrink], axis=1) + both
            acct[h] = acct[h] * shrink + bent

    def part_of(h):
        total = jnp.sum(tot[h], axis=1, keepdims=True)
        incline = jnp.sum(slp[h], axis=1, keepdims=True) * FACTOR
        inverse = 1.0 / total
        incline = incline * inverse
        main = acc[h, :, :HD] * inverse
        tangent = (acct[h] * FACTOR + acc[h, :, HD:]) * inverse - main * incline
        own_part[h, :, :HD] = main[:ROWS]
        own_part[h, :, HD:] = tangent[:ROWS]
        part_out[h, :, :HD] = main[ROWS:].astype(BF16)
        part_out[h, :, HD:] = tangent[ROWS:].astype(BF16)
        part_copy(h).start()
        lane = lax.broadcasted_iota(jnp.int32, (ROWS, HD), 1)
        stat = jnp.where(lane == 0, top[h, ROWS:, :], jnp.where(lane == 1, total[ROWS:], incline[ROWS:]))
        stat_out[h] = stat.T[0:8]
        stat_copy(h).start()
        own_stat[h, 0] = top[h, 0:ROWS, :]
        own_stat[h, 1] = jnp.broadcast_to(total[:ROWS], (ROWS, HD))
        own_stat[h, 2] = jnp.broadcast_to(incline[:ROWS], (ROWS, HD))

    def join(h):
        stat_copy(h).wait_recv()
        part_copy(h).wait_recv()
        theirs = jnp.concatenate([stat_in[h]] * (HD // 8), axis=0).T
        top1, total1, incline1 = theirs[:, 0:1], theirs[:, 1:2], theirs[:, 2:3]
        top0, total0, incline0 = own_stat[h, 0], own_stat[h, 1], own_stat[h, 2]
        high = jnp.maximum(top0, top1)
        share0 = total0 * jnp.exp2((top0 - high) * EXP_SCALE)
        share1 = total1 * jnp.exp2((top1 - high) * EXP_SCALE)
        inverse = 1.0 / (share0 + share1)
        share0 = share0 * inverse
        share1 = share1 * inverse
        incline = share0 * incline0 + share1 * incline1
        main0, tan0 = own_part[h, :, :HD], own_part[h, :, HD:]
        main1, tan1 = part_in[h, :, :HD].astype(F32), part_in[h, :, HD:].astype(F32)
        main = share0 * main0 + share1 * main1
        tangent = (share0 * (tan0 + main0 * (incline0 - incline))
                   + share1 * (tan1 + main1 * (incline1 - incline)))
        cols = pl.ds(pl.multiple_of(tp * HD, HD), HD)
        att[h, 0:ROWS, cols] = main.astype(BF16)
        att[h, ROWS:2 * ROWS, cols] = tangent.astype(BF16)
        for i in range(CHIPS + 1):
            att_copy(h, i).start()

    def project(h):
        for i in range(CHIPS, TP - 1):
            att_copy(h, i).wait_recv()
        if h == 0:
            own_w.wait()
            for i in range(TP - 1):
                w_copy(i).wait_recv()
        term = jnp.dot(att[h], wbuf[h], preferred_element_type=F32)
        if h == 0:
            proj[...] = term
        elif h < HEADS - 1:
            proj[...] += term
        else:
            out_ref[...] = proj[...] + term

    def pass_on(h, s, sends=((0, 0), (0, 1), (1, 0), (1, 1))):
        for c in range(2):
            for d in range(2):
                ring(h, s, d, c).wait_recv()
                if (c, d) in sends:
                    ring(h, s + 1, d, c).start()

    def slot(k, attending):
        def at(h):
            return k - OFFSET[h]

        for h in range(HEADS):
            s = at(h)
            if isinstance(k, int):
                if 1 <= s < STEPS - 1:
                    pass_on(h, s)
            else:
                pl.when((s >= 2) & (s < STEPS - 1))(lambda h=h, s=s: pass_on(h, s))
                pl.when(s == 1)(lambda h=h: pass_on(h, 1))
                if h < HEADS - 1:
                    pl.when(s == STEPS - 1)(lambda h=h: pass_on(h, STEPS - 1, ((0, 0), (1, 1))))
                else:
                    pl.when(s == STEPS - 2)(lambda h=h: [ring(h, STEPS, d, d).start() for d in range(2)] and None)
                    pl.when(s == STEPS - 1)(lambda h=h: pass_on(h, STEPS - 1, ()))
            if START[h] > 0:
                if isinstance(k, int):
                    if k == START[h]:
                        start_ring(h)
                else:
                    pl.when(k == START[h])(lambda h=h: start_ring(h))
        if not attending:
            return
        for h in range(HEADS):
            s = at(h)

            def inner(h=h, s=s):
                pl.when(s == 1)(lambda: attend(h, kv.at[h, 0, pl.ds(0, ROWS)], first=True))
                attend(h, kv.at[h, s])

            def last(h=h):
                ring(h, STEPS, 0, 0).wait_recv()
                ring(h, STEPS, 1, 1).wait_recv()
                attend(h, kv.at[h, 0, pl.ds(ROWS, ROWS)])
                part_of(h)

            pl.when((s >= 1) & (s < STEPS))(inner)
            pl.when(s == STEPS)(last)
        pl.when(k == STEPS + 2)(lambda: relay(0))
        for h in range(HEADS - 1):
            pl.when(k == STEPS + OFFSET[h] + 1)(lambda h=h: join(h))

    for k in range(1, 3):
        slot(k, False)
    for i in range(HEADS):
        q_copy(i).wait_recv()
    for h in range(HEADS):
        if 2 - OFFSET[h] >= 1:
            attend(h, kv.at[h, 0, pl.ds(0, ROWS)], first=True)
        for s in range(1, 3 - OFFSET[h]):
            attend(h, kv.at[h, s])

    def turn(k, carry):
        slot(k, True)
        return carry

    lax.fori_loop(3, STEPS + OFFSET[-1] + 1, turn, 0)

    project(0)
    relay(1)
    join(2)
    project(1)
    relay(2)
    project(2)

    for h in range(HEADS):
        q_copy(h).wait_send()
        part_copy(h).wait_send()
        stat_copy(h).wait_send()
        for i in range(TP - 1):
            att_copy(h, i).wait_send()
        for s in range(1, STEPS):
            for c in range(2):
                for d in range(2):
                    ring(h, s, d, c).wait_send()
        ring(h, STEPS, 0, 0).wait_send()
        ring(h, STEPS, 1, 1).wait_send()
    for i in range(TP - 1):
        w_copy(i).wait_send()


def per_device(q, qt, k, kt, v, vt, w, bias, scale, slope):
    vm = pl.BlockSpec(memory_space=pltpu.VMEM)
    dma = pltpu.SemaphoreType.DMA
    proj = pl.pallas_call(
        kernel,
        out_shape=jax.ShapeDtypeStruct((2 * ROWS, COLS), F32),
        in_specs=[pl.BlockSpec(memory_space=pl.ANY)] * 7,
        out_specs=vm,
        scratch_shapes=[
            pltpu.VMEM((HEADS, STEPS, 2 * ROWS, 4 * HD), BF16),
            pltpu.VMEM((HEADS, 2 * ROWS, 2 * HD), BF16),
            pltpu.VMEM((HEADS, TP * HD, COLS), BF16),
            pltpu.VMEM((HEADS, 2 * ROWS, TP * HD), BF16),
            pltpu.VMEM((2 * ROWS, COLS), F32),
            pltpu.VMEM((HEADS, 2 * ROWS, HD), F32),
            pltpu.VMEM((HEADS, 2 * ROWS, HD), F32),
            pltpu.VMEM((HEADS, 2 * ROWS, HD), F32),
            pltpu.VMEM((HEADS, 2 * ROWS, 2 * HD), F32),
            pltpu.VMEM((HEADS, 2 * ROWS, HD), F32),
            pltpu.VMEM((HEADS, ROWS, 2 * HD), F32),
            pltpu.VMEM((HEADS, 3, ROWS, HD), F32),
            pltpu.VMEM((HEADS, ROWS, 2 * HD), BF16),
            pltpu.VMEM((HEADS, ROWS, 2 * HD), BF16),
            pltpu.VMEM((HEADS, 8, HD), F32),
            pltpu.VMEM((HEADS, 8, HD), F32),
            dma((HEADS, STEPS, 2, 2)), dma((HEADS, STEPS, 2, 2)),
            dma((HEADS,)), dma((HEADS,)),
            dma((TP - 1,)), dma((TP - 1,)), dma,
            dma((HEADS,)), dma((HEADS,)), dma((HEADS,)), dma((HEADS,)),
            dma((HEADS, TP - 1)), dma((HEADS, TP - 1)), dma((HEADS, 6)),
        ],
        compiler_params=pltpu.CompilerParams(
            collective_id=0, has_side_effects=True, vmem_limit_bytes=63 * 2**20),
        name="attention",
    )(q, qt, k, kt, v, vt, w.reshape(HEADS, HD, -1))
    shifted = proj[:ROWS] + bias[None, :]
    block_output = (scale[None, :] * shifted).astype(BF16)
    output_tangent = (slope[None, :] * shifted + scale[None, :] * proj[ROWS:]).astype(BF16)
    return block_output, output_tangent


def solution(mesh):
    in_specs = (
        P(("dp", "ctx"), "tp"),
        P(("dp", "ctx"), "tp"),
        P(("dp", "ctx"), "tp"),
        P(("dp", "ctx"), "tp"),
        P(("dp", "ctx"), "tp"),
        P(("dp", "ctx"), "tp"),
        P("tp", None),
        P("tp"),
        P(("dp", "tp")),
        P(("dp", "tp")),
    )
    out_specs = (P(("dp", "ctx"), "tp"), P(("dp", "ctx"), "tp"))
    return jax.shard_map(
        per_device, mesh=mesh, in_specs=in_specs, out_specs=out_specs, check_vma=False
    )
```

```python
import math

import jax
import jax.numpy as jnp
from jax import lax
from jax.experimental import pallas as pl
from jax.experimental.pallas import tpu as pltpu
from jax.sharding import PartitionSpec as P

HD = 128
HEADS = 3
ROWS = 128
HALF = ROWS // 2
RING = 16
STEPS = RING // 2
OFFSET = (0, 2, 4)
START = (0, 0, 2)
TP = 8
CHIPS = TP // 2 - 1
COLS = 640
FACTOR = HD ** (-0.5)
EXP_SCALE = FACTOR * math.log2(math.e)
MESH = pl.DeviceIdType.MESH
F32 = jnp.float32
BF16 = jnp.bfloat16


def dot_nt(a, b):
    return lax.dot_general(a, b, (((1,), (1,)), ((), ())), preferred_element_type=F32)


def kernel(
    q_ref, qt_ref, k_ref, kt_ref, v_ref, vt_ref, w_ref, out_ref,
    kv, qbuf, wbuf, att, proj, top, tot, slp, acc, acct,
    own_part, own_stat, part_out, part_in, stat_out, stat_in,
    ring_send, ring_recv, q_send, q_recv, w_send, w_recv, w_own,
    part_ssem, part_rsem, stat_ssem, stat_rsem, att_send, att_recv, load_sem,
):
    ctx = lax.axis_index("ctx")
    tp = lax.axis_index("tp")
    z, y = ctx // 2, ctx % 2
    right = lax.rem(z + 1, RING) * 2 + y
    left = lax.rem(z + RING - 1, RING) * 2 + y
    far_right = lax.rem(z + 2, RING) * 2 + y
    far_left = lax.rem(z + RING - 2, RING) * 2 + y
    partner = z * 2 + (1 - y)
    sibling = tp + 1 - 2 * lax.rem(tp, 2)
    peers = [lax.rem(tp + i, TP) for i in range(1, TP)]

    barrier = pltpu.get_barrier_semaphore()
    for where in [{"ctx": c} for c in (right, left, far_right, far_left, partner)] + [{"tp": p} for p in peers]:
        pl.semaphore_signal(barrier, inc=1, device_id=where, device_id_type=MESH)

    def load_copies(h):
        cols = pl.ds(h * HD, HD)
        targets = [(ref, kv.at[h, 0, pl.ds(0, ROWS), pl.ds(i * HD, HD)])
                   for i, ref in enumerate((k_ref, kt_ref, v_ref, vt_ref))]
        targets += [(ref, qbuf.at[h, pl.ds(0, ROWS), pl.ds(i * HD, HD)])
                    for i, ref in enumerate((qt_ref, q_ref))]
        return [pltpu.make_async_copy(ref.at[:, cols], target, load_sem.at[h, i])
                for i, (ref, target) in enumerate(targets)]

    for h in range(HEADS):
        for copy in load_copies(h):
            copy.start()

    def ring(h, s, d, c):
        lo = c * HALF
        targets = (right, left)
        if isinstance(s, int) and s == STEPS:
            back = 1
            if h == HEADS - 1:
                back, targets = 2, (far_right, far_left)
            src = kv.at[h, STEPS - back, pl.ds(d * ROWS + lo, HALF)]
            dst = kv.at[h, 0, pl.ds(ROWS + lo, HALF)]
        else:
            first = isinstance(s, int) and s == 1
            src = kv.at[h, s - 1, pl.ds((0 if first else d * ROWS) + lo, HALF)]
            dst = kv.at[h, s, pl.ds(d * ROWS + lo, HALF)]
        return pltpu.make_async_remote_copy(
            src_ref=src, dst_ref=dst,
            send_sem=ring_send.at[h, s - 1, d, c], recv_sem=ring_recv.at[h, s - 1, d, c],
            device_id={"ctx": targets[d]}, device_id_type=MESH)

    def start_ring(h):
        for c in range(2):
            for d in range(2):
                ring(h, 1, d, c).start()

    def q_copy(h):
        return pltpu.make_async_remote_copy(
            src_ref=qbuf.at[h, pl.ds(0, ROWS)], dst_ref=qbuf.at[h, pl.ds(ROWS, ROWS)],
            send_sem=q_send.at[h], recv_sem=q_recv.at[h],
            device_id={"ctx": partner}, device_id_type=MESH)

    def w_copy(i):
        peer = lax.rem(tp + i + 1, TP)
        return pltpu.make_async_remote_copy(
            src_ref=w_ref.at[:, :, pl.ds(pl.multiple_of(peer * COLS, COLS), COLS)],
            dst_ref=wbuf.at[:, pl.ds(pl.multiple_of(tp * HD, HD), HD), :],
            send_sem=w_send.at[i], recv_sem=w_recv.at[i],
            device_id={"tp": peer}, device_id_type=MESH)

    def att_copy(h, r, i):
        owner = tp if i <= CHIPS else lax.rem(tp + TP - 2 * (i - CHIPS), TP)
        peer = lax.rem(tp + 2 * (i + 1), TP) if i < CHIPS else sibling
        part = att.at[h, pl.ds(r * ROWS, ROWS), pl.ds(pl.multiple_of(owner * HD, HD), HD)]
        return pltpu.make_async_remote_copy(
            src_ref=part, dst_ref=part,
            send_sem=att_send.at[h, r, i], recv_sem=att_recv.at[h, r, i],
            device_id={"tp": peer}, device_id_type=MESH)

    def relay(h):
        for r in range(2):
            for i in (0, 2, 1):
                att_copy(h, r, i).wait_recv()
                att_copy(h, r, CHIPS + 1 + i).start()

    def part_copy(h, r):
        rows = pl.ds(r * HALF, HALF)
        return pltpu.make_async_remote_copy(
            src_ref=part_out.at[h, rows], dst_ref=part_in.at[h, rows],
            send_sem=part_ssem.at[h, r], recv_sem=part_rsem.at[h, r],
            device_id={"ctx": partner}, device_id_type=MESH)

    def stat_copy(h):
        return pltpu.make_async_remote_copy(
            src_ref=stat_out.at[h], dst_ref=stat_in.at[h],
            send_sem=stat_ssem.at[h], recv_sem=stat_rsem.at[h],
            device_id={"ctx": partner}, device_id_type=MESH)

    own_w = pltpu.make_async_copy(
        w_ref.at[:, :, pl.ds(pl.multiple_of(tp * COLS, COLS), COLS)],
        wbuf.at[:, pl.ds(pl.multiple_of(tp * HD, HD), HD), :], w_own)

    pl.semaphore_wait(barrier, 5 + TP - 1)
    for h in range(HEADS):
        for copy in load_copies(h):
            copy.wait()
        if START[h] == 0:
            start_ring(h)
    for h in range(HEADS):
        q_copy(h).start()
    for i in range(TP - 1):
        w_copy(i).start()
    own_w.start()

    def attend(h, block, first=False):
        pair = qbuf[h]
        keys = block[:, 0:2 * HD]
        scores = dot_nt(pair[:, HD:], keys[:, :HD])
        tilt = dot_nt(pair, keys)
        count = scores.shape[1]
        peak = jnp.max(scores, axis=1, keepdims=True)
        if first:
            new = jnp.broadcast_to(peak, (2 * ROWS, HD))
        else:
            old = top[h]
            new = jnp.maximum(old, peak)
            shrink = jnp.exp2((old - new) * EXP_SCALE)
        top[h] = new
        wide = jnp.concatenate([new] * (count // HD), axis=1) if count > HD else new
        weights = jnp.exp2((scores - wide) * EXP_SCALE)
        slanted = weights * tilt
        folded, tilted = weights[:, :HD], slanted[:, :HD]
        for i in range(1, count // HD):
            folded = folded + weights[:, i * HD:(i + 1) * HD]
            tilted = tilted + slanted[:, i * HD:(i + 1) * HD]
        values = block[:, 2 * HD:]
        both = jnp.dot(weights.astype(BF16), values, preferred_element_type=F32)
        bent = jnp.dot(slanted.astype(BF16), values[:, :HD], preferred_element_type=F32)
        if first:
            tot[h] = folded
            slp[h] = tilted
            acc[h] = both
            acct[h] = bent
        else:
            tot[h] = tot[h] * shrink + folded
            slp[h] = slp[h] * shrink + tilted
            acc[h] = acc[h] * jnp.concatenate([shrink, shrink], axis=1) + both
            acct[h] = acct[h] * shrink + bent

    def part_of(h):
        total = jnp.sum(tot[h], axis=1, keepdims=True)
        inverse = 1.0 / total
        incline = jnp.sum(slp[h], axis=1, keepdims=True) * FACTOR * inverse
        lane = lax.broadcasted_iota(jnp.int32, (ROWS, HD), 1)
        stat = jnp.where(lane == 0, top[h, ROWS:, :], jnp.where(lane == 1, total[ROWS:], incline[ROWS:]))
        stat_out[h] = stat.T[0:8]
        stat_copy(h).start()

        def piece(rows):
            main = acc[h, rows, :HD] * inverse[rows]
            tangent = (acct[h, rows] * FACTOR + acc[h, rows, HD:]) * inverse[rows] - main * incline[rows]
            return main, tangent

        for r in range(2):
            rows = slice(r * HALF, (r + 1) * HALF)
            main, tangent = piece(slice(ROWS + r * HALF, ROWS + (r + 1) * HALF))
            part_out[h, rows, :HD] = main.astype(BF16)
            part_out[h, rows, HD:] = tangent.astype(BF16)
            part_copy(h, r).start()
        main, tangent = piece(slice(0, ROWS))
        own_part[h, :, :HD] = main
        own_part[h, :, HD:] = tangent
        own_stat[h, 0] = top[h, 0:ROWS, :]
        own_stat[h, 1] = jnp.broadcast_to(total[:ROWS], (ROWS, HD))
        own_stat[h, 2] = jnp.broadcast_to(incline[:ROWS], (ROWS, HD))

    def join(h):
        stat_copy(h).wait_recv()
        theirs = jnp.concatenate([stat_in[h]] * (HD // 8), axis=0).T
        top1, total1, incline1 = theirs[:, 0:1], theirs[:, 1:2], theirs[:, 2:3]
        top0, total0, incline0 = own_stat[h, 0], own_stat[h, 1], own_stat[h, 2]
        high = jnp.maximum(top0, top1)
        share0 = total0 * jnp.exp2((top0 - high) * EXP_SCALE)
        share1 = total1 * jnp.exp2((top1 - high) * EXP_SCALE)
        inverse = 1.0 / (share0 + share1)
        share0 = share0 * inverse
        share1 = share1 * inverse
        incline = share0 * incline0 + share1 * incline1
        cols = pl.ds(pl.multiple_of(tp * HD, HD), HD)
        for r in range(2):
            rows = slice(r * HALF, (r + 1) * HALF)
            part_copy(h, r).wait_recv()
            main0, tan0 = own_part[h, rows, :HD], own_part[h, rows, HD:]
            main1, tan1 = part_in[h, rows, :HD].astype(F32), part_in[h, rows, HD:].astype(F32)
            part0, part1, tilt = share0[rows], share1[rows], incline[rows]
            main = part0 * main0 + part1 * main1
            tangent = (part0 * (tan0 + main0 * (incline0[rows] - tilt))
                       + part1 * (tan1 + main1 * (incline1[rows] - tilt)))
            att[h, r * ROWS:r * ROWS + HALF, cols] = main.astype(BF16)
            att[h, r * ROWS + HALF:(r + 1) * ROWS, cols] = tangent.astype(BF16)
            for i in (1, 0, 2, CHIPS):
                att_copy(h, r, i).start()

    def project(h):
        if h == 0:
            own_w.wait()
            for i in range(TP - 1):
                w_copy(i).wait_recv()
        for r in range(2):
            rows = slice(r * ROWS, (r + 1) * ROWS)
            for i in range(CHIPS, TP - 1):
                att_copy(h, r, i).wait_recv()
            term = jnp.dot(att[h, rows], wbuf[h], preferred_element_type=F32)
            if h == 0:
                proj[rows] = term
            elif h < HEADS - 1:
                proj[rows] += term
            else:
                term = proj[rows] + term
                out_ref[r * HALF:(r + 1) * HALF] = term[:HALF]
                out_ref[ROWS + r * HALF:ROWS + (r + 1) * HALF] = term[HALF:]

    def pass_on(h, s, sends=((0, 0), (0, 1), (1, 0), (1, 1))):
        for c in range(2):
            for d in range(2):
                ring(h, s, d, c).wait_recv()
                if (c, d) in sends:
                    ring(h, s + 1, d, c).start()

    def slot(k, attending):
        def at(h):
            return k - OFFSET[h]

        for h in range(HEADS):
            s = at(h)
            if isinstance(k, int):
                if 1 <= s < STEPS - 1:
                    pass_on(h, s)
            else:
                pl.when((s >= 2) & (s < STEPS - 1))(lambda h=h, s=s: pass_on(h, s))
                pl.when(s == 1)(lambda h=h: pass_on(h, 1))
                if h < HEADS - 1:
                    pl.when(s == STEPS - 1)(lambda h=h: pass_on(h, STEPS - 1, ((0, 0), (1, 1))))
                else:
                    pl.when(s == STEPS - 2)(lambda h=h: [ring(h, STEPS, d, d).start() for d in range(2)] and None)
                    pl.when(s == STEPS - 1)(lambda h=h: pass_on(h, STEPS - 1, ()))
            if START[h] > 0:
                if isinstance(k, int):
                    if k == START[h]:
                        start_ring(h)
                else:
                    pl.when(k == START[h])(lambda h=h: start_ring(h))
        if not attending:
            return
        for h in range(HEADS):
            s = at(h)

            def inner(h=h, s=s):
                pl.when(s == 1)(lambda: attend(h, kv.at[h, 0, pl.ds(0, ROWS)], first=True))
                attend(h, kv.at[h, s])

            def last(h=h):
                ring(h, STEPS, 0, 0).wait_recv()
                ring(h, STEPS, 1, 1).wait_recv()
                attend(h, kv.at[h, 0, pl.ds(ROWS, ROWS)])
                part_of(h)

            pl.when((s >= 1) & (s < STEPS))(inner)
            pl.when(s == STEPS)(last)
        pl.when(k == STEPS + 2)(lambda: relay(0))
        for h in range(HEADS - 1):
            pl.when(k == STEPS + OFFSET[h] + 1)(lambda h=h: join(h))

    for k in range(1, 3):
        slot(k, False)
    for i in range(HEADS):
        q_copy(i).wait_recv()
    for h in range(HEADS):
        if 2 - OFFSET[h] >= 1:
            attend(h, kv.at[h, 0, pl.ds(0, ROWS)], first=True)
        for s in range(1, 3 - OFFSET[h]):
            attend(h, kv.at[h, s])

    def turn(k, carry):
        slot(k, True)
        return carry

    lax.fori_loop(3, STEPS + OFFSET[-1] + 1, turn, 0)

    project(0)
    relay(1)
    for h in range(HEADS):
        q_copy(h).wait_send()
        for r in range(2):
            part_copy(h, r).wait_send()
        stat_copy(h).wait_send()
        for s in range(1, STEPS):
            for c in range(2):
                for d in range(2):
                    ring(h, s, d, c).wait_send()
        ring(h, STEPS, 0, 0).wait_send()
        ring(h, STEPS, 1, 1).wait_send()
    for i in range(TP - 1):
        w_copy(i).wait_send()
    join(2)
    project(1)
    relay(2)
    project(2)

    for h in range(HEADS):
        for r in range(2):
            for i in range(TP - 1):
                att_copy(h, r, i).wait_send()


def per_device(q, qt, k, kt, v, vt, w, bias, scale, slope):
    vm = pl.BlockSpec(memory_space=pltpu.VMEM)
    dma = pltpu.SemaphoreType.DMA
    proj = pl.pallas_call(
        kernel,
        out_shape=jax.ShapeDtypeStruct((2 * ROWS, COLS), F32),
        in_specs=[pl.BlockSpec(memory_space=pl.ANY)] * 7,
        out_specs=vm,
        scratch_shapes=[
            pltpu.VMEM((HEADS, STEPS, 2 * ROWS, 4 * HD), BF16),
            pltpu.VMEM((HEADS, 2 * ROWS, 2 * HD), BF16),
            pltpu.VMEM((HEADS, TP * HD, COLS), BF16),
            pltpu.VMEM((HEADS, 2 * ROWS, TP * HD), BF16),
            pltpu.VMEM((2 * ROWS, COLS), F32),
            pltpu.VMEM((HEADS, 2 * ROWS, HD), F32),
            pltpu.VMEM((HEADS, 2 * ROWS, HD), F32),
            pltpu.VMEM((HEADS, 2 * ROWS, HD), F32),
            pltpu.VMEM((HEADS, 2 * ROWS, 2 * HD), F32),
            pltpu.VMEM((HEADS, 2 * ROWS, HD), F32),
            pltpu.VMEM((HEADS, ROWS, 2 * HD), F32),
            pltpu.VMEM((HEADS, 3, ROWS, HD), F32),
            pltpu.VMEM((HEADS, ROWS, 2 * HD), BF16),
            pltpu.VMEM((HEADS, ROWS, 2 * HD), BF16),
            pltpu.VMEM((HEADS, 8, HD), F32),
            pltpu.VMEM((HEADS, 8, HD), F32),
            dma((HEADS, STEPS, 2, 2)), dma((HEADS, STEPS, 2, 2)),
            dma((HEADS,)), dma((HEADS,)),
            dma((TP - 1,)), dma((TP - 1,)), dma,
            dma((HEADS, 2)), dma((HEADS, 2)), dma((HEADS,)), dma((HEADS,)),
            dma((HEADS, 2, TP - 1)), dma((HEADS, 2, TP - 1)), dma((HEADS, 6)),
        ],
        compiler_params=pltpu.CompilerParams(
            collective_id=0, has_side_effects=True, vmem_limit_bytes=63 * 2**20),
        name="attention",
    )(q, qt, k, kt, v, vt, w.reshape(HEADS, HD, -1))
    shifted = proj[:ROWS] + bias[None, :]
    block_output = (scale[None, :] * shifted).astype(BF16)
    output_tangent = (slope[None, :] * shifted + scale[None, :] * proj[ROWS:]).astype(BF16)
    return block_output, output_tangent


def solution(mesh):
    in_specs = (
        P(("dp", "ctx"), "tp"),
        P(("dp", "ctx"), "tp"),
        P(("dp", "ctx"), "tp"),
        P(("dp", "ctx"), "tp"),
        P(("dp", "ctx"), "tp"),
        P(("dp", "ctx"), "tp"),
        P("tp", None),
        P("tp"),
        P(("dp", "tp")),
        P(("dp", "tp")),
    )
    out_specs = (P(("dp", "ctx"), "tp"), P(("dp", "ctx"), "tp"))
    return jax.shard_map(
        per_device, mesh=mesh, in_specs=in_specs, out_specs=out_specs, check_vma=False
    )
```

```python
import math

import jax
import jax.numpy as jnp
from jax import lax
from jax.experimental import pallas as pl
from jax.experimental.pallas import tpu as pltpu
from jax.sharding import PartitionSpec as P

HD = 128
HEADS = 3
ROWS = 128
HALF = ROWS // 2
RING = 16
STEPS = RING // 2
OFFSET = (0, 2, 4)
START = (0, 0, 2)
TP = 8
CHIPS = TP // 2 - 1
COLS = 640
FACTOR = HD ** (-0.5)
EXP_SCALE = FACTOR * math.log2(math.e)
MESH = pl.DeviceIdType.MESH
F32 = jnp.float32
BF16 = jnp.bfloat16


def dot_nt(a, b):
    return lax.dot_general(a, b, (((1,), (1,)), ((), ())), preferred_element_type=F32)


def kernel(
    q_ref, qt_ref, k_ref, kt_ref, v_ref, vt_ref, w_ref, out_ref,
    kv, qbuf, wbuf, att, proj, top, tot, slp, acc, acct,
    own_part, own_stat, part_out, part_in, stat_out, stat_in,
    ring_send, ring_recv, q_send, q_recv, w_send, w_recv, w_own,
    part_ssem, part_rsem, stat_ssem, stat_rsem, att_send, att_recv, load_sem,
):
    ctx = lax.axis_index("ctx")
    tp = lax.axis_index("tp")
    z, y = ctx // 2, ctx % 2
    right = lax.rem(z + 1, RING) * 2 + y
    left = lax.rem(z + RING - 1, RING) * 2 + y
    far_right = lax.rem(z + 2, RING) * 2 + y
    far_left = lax.rem(z + RING - 2, RING) * 2 + y
    partner = z * 2 + (1 - y)
    sibling = tp + 1 - 2 * lax.rem(tp, 2)
    peers = [lax.rem(tp + i, TP) for i in range(1, TP)]

    barrier = pltpu.get_barrier_semaphore()
    for where in [{"ctx": c} for c in (right, left, far_right, far_left, partner)] + [{"tp": p} for p in peers]:
        pl.semaphore_signal(barrier, inc=1, device_id=where, device_id_type=MESH)

    def load_copies(h):
        cols = pl.ds(h * HD, HD)
        targets = [(ref, kv.at[h, 0, pl.ds(0, ROWS), pl.ds(i * HD, HD)])
                   for i, ref in enumerate((k_ref, kt_ref, v_ref, vt_ref))]
        targets += [(ref, qbuf.at[h, pl.ds(0, ROWS), pl.ds(i * HD, HD)])
                    for i, ref in enumerate((qt_ref, q_ref))]
        return [pltpu.make_async_copy(ref.at[:, cols], target, load_sem.at[h, i])
                for i, (ref, target) in enumerate(targets)]

    for h in range(HEADS):
        for copy in load_copies(h):
            copy.start()

    def ring(h, s, d, c):
        lo = c * HALF
        targets = (right, left)
        if isinstance(s, int) and s == STEPS:
            back = 1
            if h == HEADS - 1:
                back, targets = 2, (far_right, far_left)
            src = kv.at[h, STEPS - back, pl.ds(d * ROWS + lo, HALF)]
            dst = kv.at[h, 0, pl.ds(ROWS + lo, HALF)]
        else:
            first = isinstance(s, int) and s == 1
            src = kv.at[h, s - 1, pl.ds((0 if first else d * ROWS) + lo, HALF)]
            dst = kv.at[h, s, pl.ds(d * ROWS + lo, HALF)]
        return pltpu.make_async_remote_copy(
            src_ref=src, dst_ref=dst,
            send_sem=ring_send.at[h, s - 1, d, c], recv_sem=ring_recv.at[h, s - 1, d, c],
            device_id={"ctx": targets[d]}, device_id_type=MESH)

    def start_ring(h):
        for c in range(2):
            for d in range(2):
                ring(h, 1, d, c).start()

    def q_copy(h):
        return pltpu.make_async_remote_copy(
            src_ref=qbuf.at[h, pl.ds(0, ROWS)], dst_ref=qbuf.at[h, pl.ds(ROWS, ROWS)],
            send_sem=q_send.at[h], recv_sem=q_recv.at[h],
            device_id={"ctx": partner}, device_id_type=MESH)

    def w_copy(i):
        peer = lax.rem(tp + i + 1, TP)
        return pltpu.make_async_remote_copy(
            src_ref=w_ref.at[:, :, pl.ds(pl.multiple_of(peer * COLS, COLS), COLS)],
            dst_ref=wbuf.at[:, pl.ds(pl.multiple_of(tp * HD, HD), HD), :],
            send_sem=w_send.at[i], recv_sem=w_recv.at[i],
            device_id={"tp": peer}, device_id_type=MESH)

    def att_copy(h, r, i):
        owner = tp if i <= CHIPS else lax.rem(tp + TP - 2 * (i - CHIPS), TP)
        peer = lax.rem(tp + 2 * (i + 1), TP) if i < CHIPS else sibling
        part = att.at[h, pl.ds(r * ROWS, ROWS), pl.ds(pl.multiple_of(owner * HD, HD), HD)]
        return pltpu.make_async_remote_copy(
            src_ref=part, dst_ref=part,
            send_sem=att_send.at[h, r, i], recv_sem=att_recv.at[h, r, i],
            device_id={"tp": peer}, device_id_type=MESH)

    def relay(h):
        for r in range(2):
            for i in (0, 2, 1):
                att_copy(h, r, i).wait_recv()
                att_copy(h, r, CHIPS + 1 + i).start()

    def part_copy(h, r):
        rows = pl.ds(r * HALF, HALF)
        return pltpu.make_async_remote_copy(
            src_ref=part_out.at[h, rows], dst_ref=part_in.at[h, rows],
            send_sem=part_ssem.at[h, r], recv_sem=part_rsem.at[h, r],
            device_id={"ctx": partner}, device_id_type=MESH)

    def stat_copy(h):
        return pltpu.make_async_remote_copy(
            src_ref=stat_out.at[h], dst_ref=stat_in.at[h],
            send_sem=stat_ssem.at[h], recv_sem=stat_rsem.at[h],
            device_id={"ctx": partner}, device_id_type=MESH)

    own_w = pltpu.make_async_copy(
        w_ref.at[:, :, pl.ds(pl.multiple_of(tp * COLS, COLS), COLS)],
        wbuf.at[:, pl.ds(pl.multiple_of(tp * HD, HD), HD), :], w_own)

    pl.semaphore_wait(barrier, 5 + TP - 1)
    for h in range(HEADS):
        for copy in load_copies(h):
            copy.wait()
        if START[h] == 0:
            start_ring(h)
    for h in range(HEADS):
        q_copy(h).start()

    def attend(h, block, first=False):
        pair = qbuf[h]
        keys = block[:, 0:2 * HD]
        scores = dot_nt(pair[:, HD:], keys[:, :HD])
        tilt = dot_nt(pair, keys)
        count = scores.shape[1]
        peak = jnp.max(scores, axis=1, keepdims=True)
        if first:
            new = jnp.broadcast_to(peak, (2 * ROWS, HD))
        else:
            old = top[h]
            new = jnp.maximum(old, peak)
            shrink = jnp.exp2((old - new) * EXP_SCALE)
        top[h] = new
        wide = jnp.concatenate([new] * (count // HD), axis=1) if count > HD else new
        weights = jnp.exp2((scores - wide) * EXP_SCALE)
        slanted = weights * tilt
        folded, tilted = weights[:, :HD], slanted[:, :HD]
        for i in range(1, count // HD):
            folded = folded + weights[:, i * HD:(i + 1) * HD]
            tilted = tilted + slanted[:, i * HD:(i + 1) * HD]
        values = block[:, 2 * HD:]
        both = jnp.dot(weights.astype(BF16), values, preferred_element_type=F32)
        bent = jnp.dot(slanted.astype(BF16), values[:, :HD], preferred_element_type=F32)
        if first:
            tot[h] = folded
            slp[h] = tilted
            acc[h] = both
            acct[h] = bent
        else:
            tot[h] = tot[h] * shrink + folded
            slp[h] = slp[h] * shrink + tilted
            acc[h] = acc[h] * jnp.concatenate([shrink, shrink], axis=1) + both
            acct[h] = acct[h] * shrink + bent

    def part_of(h):
        total = jnp.sum(tot[h], axis=1, keepdims=True)
        inverse = 1.0 / total
        incline = jnp.sum(slp[h], axis=1, keepdims=True) * FACTOR * inverse
        lane = lax.broadcasted_iota(jnp.int32, (ROWS, HD), 1)
        stat = jnp.where(lane == 0, top[h, ROWS:, :], jnp.where(lane == 1, total[ROWS:], incline[ROWS:]))
        stat_out[h] = stat.T[0:8]
        stat_copy(h).start()

        def piece(rows):
            main = acc[h, rows, :HD] * inverse[rows]
            tangent = (acct[h, rows] * FACTOR + acc[h, rows, HD:]) * inverse[rows] - main * incline[rows]
            return main, tangent

        for r in range(2):
            rows = slice(r * HALF, (r + 1) * HALF)
            main, tangent = piece(slice(ROWS + r * HALF, ROWS + (r + 1) * HALF))
            part_out[h, rows, :HD] = main.astype(BF16)
            part_out[h, rows, HD:] = tangent.astype(BF16)
            part_copy(h, r).start()
        main, tangent = piece(slice(0, ROWS))
        own_part[h, :, :HD] = main
        own_part[h, :, HD:] = tangent
        own_stat[h, 0] = top[h, 0:ROWS, :]
        own_stat[h, 1] = jnp.broadcast_to(total[:ROWS], (ROWS, HD))
        own_stat[h, 2] = jnp.broadcast_to(incline[:ROWS], (ROWS, HD))

    def join(h):
        stat_copy(h).wait_recv()
        theirs = jnp.concatenate([stat_in[h]] * (HD // 8), axis=0).T
        top1, total1, incline1 = theirs[:, 0:1], theirs[:, 1:2], theirs[:, 2:3]
        top0, total0, incline0 = own_stat[h, 0], own_stat[h, 1], own_stat[h, 2]
        high = jnp.maximum(top0, top1)
        share0 = total0 * jnp.exp2((top0 - high) * EXP_SCALE)
        share1 = total1 * jnp.exp2((top1 - high) * EXP_SCALE)
        inverse = 1.0 / (share0 + share1)
        share0 = share0 * inverse
        share1 = share1 * inverse
        incline = share0 * incline0 + share1 * incline1
        cols = pl.ds(pl.multiple_of(tp * HD, HD), HD)
        for r in range(2):
            rows = slice(r * HALF, (r + 1) * HALF)
            part_copy(h, r).wait_recv()
            main0, tan0 = own_part[h, rows, :HD], own_part[h, rows, HD:]
            main1, tan1 = part_in[h, rows, :HD].astype(F32), part_in[h, rows, HD:].astype(F32)
            part0, part1, tilt = share0[rows], share1[rows], incline[rows]
            main = part0 * main0 + part1 * main1
            tangent = (part0 * (tan0 + main0 * (incline0[rows] - tilt))
                       + part1 * (tan1 + main1 * (incline1[rows] - tilt)))
            att[h, r * ROWS:r * ROWS + HALF, cols] = main.astype(BF16)
            att[h, r * ROWS + HALF:(r + 1) * ROWS, cols] = tangent.astype(BF16)
            for i in (1, 0, 2, CHIPS):
                att_copy(h, r, i).start()

    def project(h):
        if h == 0:
            own_w.wait()
            for i in range(TP - 1):
                w_copy(i).wait_recv()
        for r in range(2):
            rows = slice(r * ROWS, (r + 1) * ROWS)
            for i in range(CHIPS, TP - 1):
                att_copy(h, r, i).wait_recv()
            term = jnp.dot(att[h, rows], wbuf[h], preferred_element_type=F32)
            if h == 0:
                proj[rows] = term
            elif h < HEADS - 1:
                proj[rows] += term
            else:
                term = proj[rows] + term
                out_ref[r * HALF:(r + 1) * HALF] = term[:HALF]
                out_ref[ROWS + r * HALF:ROWS + (r + 1) * HALF] = term[HALF:]

    def pass_on(h, s, sends=((0, 0), (0, 1), (1, 0), (1, 1))):
        for c in range(2):
            for d in range(2):
                ring(h, s, d, c).wait_recv()
                if (c, d) in sends:
                    ring(h, s + 1, d, c).start()

    def slot(k, attending):
        def at(h):
            return k - OFFSET[h]

        for h in range(HEADS):
            s = at(h)
            if isinstance(k, int):
                if 1 <= s < STEPS - 1:
                    pass_on(h, s)
            else:
                pl.when((s >= 2) & (s < STEPS - 1))(lambda h=h, s=s: pass_on(h, s))
                pl.when(s == 1)(lambda h=h: pass_on(h, 1))
                if h < HEADS - 1:
                    pl.when(s == STEPS - 1)(lambda h=h: pass_on(h, STEPS - 1, ((0, 0), (1, 1))))
                else:
                    pl.when(s == STEPS - 2)(lambda h=h: [ring(h, STEPS, d, d).start() for d in range(2)] and None)
                    pl.when(s == STEPS - 1)(lambda h=h: pass_on(h, STEPS - 1, ()))
            if START[h] > 0:
                if isinstance(k, int):
                    if k == START[h]:
                        start_ring(h)
                else:
                    pl.when(k == START[h])(lambda h=h: start_ring(h))
        if not attending:
            return
        for h in range(HEADS):
            s = at(h)

            def inner(h=h, s=s):
                pl.when(s == 1)(lambda: attend(h, kv.at[h, 0, pl.ds(0, ROWS)], first=True))
                attend(h, kv.at[h, s])

            def last(h=h):
                ring(h, STEPS, 0, 0).wait_recv()
                ring(h, STEPS, 1, 1).wait_recv()
                attend(h, kv.at[h, 0, pl.ds(ROWS, ROWS)])
                part_of(h)

            pl.when((s >= 1) & (s < STEPS))(inner)
            pl.when(s == STEPS)(last)
        pl.when(k == STEPS + 2)(lambda: relay(0))
        for h in range(HEADS - 1):
            pl.when(k == STEPS + OFFSET[h] + 1)(lambda h=h: join(h))

    slot(1, False)
    for i in range(TP - 1):
        w_copy(i).start()
    own_w.start()
    slot(2, False)
    for i in range(HEADS):
        q_copy(i).wait_recv()
    for h in range(HEADS):
        if 2 - OFFSET[h] >= 1:
            attend(h, kv.at[h, 0, pl.ds(0, ROWS)], first=True)
        for s in range(1, 3 - OFFSET[h]):
            attend(h, kv.at[h, s])

    def turn(k, carry):
        slot(k, True)
        return carry

    lax.fori_loop(3, STEPS + OFFSET[-1] + 1, turn, 0)

    project(0)
    relay(1)
    for h in range(HEADS):
        q_copy(h).wait_send()
        for r in range(2):
            part_copy(h, r).wait_send()
        stat_copy(h).wait_send()
        for s in range(1, STEPS):
            for c in range(2):
                for d in range(2):
                    ring(h, s, d, c).wait_send()
        ring(h, STEPS, 0, 0).wait_send()
        ring(h, STEPS, 1, 1).wait_send()
    for i in range(TP - 1):
        w_copy(i).wait_send()
    join(2)
    project(1)
    relay(2)
    project(2)

    for h in range(HEADS):
        for r in range(2):
            for i in range(TP - 1):
                att_copy(h, r, i).wait_send()


def per_device(q, qt, k, kt, v, vt, w, bias, scale, slope):
    vm = pl.BlockSpec(memory_space=pltpu.VMEM)
    dma = pltpu.SemaphoreType.DMA
    proj = pl.pallas_call(
        kernel,
        out_shape=jax.ShapeDtypeStruct((2 * ROWS, COLS), F32),
        in_specs=[pl.BlockSpec(memory_space=pl.ANY)] * 7,
        out_specs=vm,
        scratch_shapes=[
            pltpu.VMEM((HEADS, STEPS, 2 * ROWS, 4 * HD), BF16),
            pltpu.VMEM((HEADS, 2 * ROWS, 2 * HD), BF16),
            pltpu.VMEM((HEADS, TP * HD, COLS), BF16),
            pltpu.VMEM((HEADS, 2 * ROWS, TP * HD), BF16),
            pltpu.VMEM((2 * ROWS, COLS), F32),
            pltpu.VMEM((HEADS, 2 * ROWS, HD), F32),
            pltpu.VMEM((HEADS, 2 * ROWS, HD), F32),
            pltpu.VMEM((HEADS, 2 * ROWS, HD), F32),
            pltpu.VMEM((HEADS, 2 * ROWS, 2 * HD), F32),
            pltpu.VMEM((HEADS, 2 * ROWS, HD), F32),
            pltpu.VMEM((HEADS, ROWS, 2 * HD), F32),
            pltpu.VMEM((HEADS, 3, ROWS, HD), F32),
            pltpu.VMEM((HEADS, ROWS, 2 * HD), BF16),
            pltpu.VMEM((HEADS, ROWS, 2 * HD), BF16),
            pltpu.VMEM((HEADS, 8, HD), F32),
            pltpu.VMEM((HEADS, 8, HD), F32),
            dma((HEADS, STEPS, 2, 2)), dma((HEADS, STEPS, 2, 2)),
            dma((HEADS,)), dma((HEADS,)),
            dma((TP - 1,)), dma((TP - 1,)), dma,
            dma((HEADS, 2)), dma((HEADS, 2)), dma((HEADS,)), dma((HEADS,)),
            dma((HEADS, 2, TP - 1)), dma((HEADS, 2, TP - 1)), dma((HEADS, 6)),
        ],
        compiler_params=pltpu.CompilerParams(
            collective_id=0, has_side_effects=True, vmem_limit_bytes=63 * 2**20),
        name="attention",
    )(q, qt, k, kt, v, vt, w.reshape(HEADS, HD, -1))
    shifted = proj[:ROWS] + bias[None, :]
    block_output = (scale[None, :] * shifted).astype(BF16)
    output_tangent = (slope[None, :] * shifted + scale[None, :] * proj[ROWS:]).astype(BF16)
    return block_output, output_tangent


def solution(mesh):
    in_specs = (
        P(("dp", "ctx"), "tp"),
        P(("dp", "ctx"), "tp"),
        P(("dp", "ctx"), "tp"),
        P(("dp", "ctx"), "tp"),
        P(("dp", "ctx"), "tp"),
        P(("dp", "ctx"), "tp"),
        P("tp", None),
        P("tp"),
        P(("dp", "tp")),
        P(("dp", "tp")),
    )
    out_specs = (P(("dp", "ctx"), "tp"), P(("dp", "ctx"), "tp"))
    return jax.shard_map(
        per_device, mesh=mesh, in_specs=in_specs, out_specs=out_specs, check_vma=False
    )
```
